32 devices in a mesh: dp: 4 (over y, x), expert: 8 (over z, core).
Axes of the slice: x: 2, y: 2, z: 4, core: 2. Of those that a mesh axis runs over, the one named last changes fastest.
Arguments:
- cotangent: bfloat16 [4096, 5120], P(('dp', 'expert')), may hold values from -6 to 6
- route_weights: float32 [4096, 6], P(('dp', 'expert')), may hold values from 0.05 to 1
- token_experts: int32 [4096, 6], P(('dp', 'expert')), may hold values from 0 to 159, as said below
- saved_hidden: bfloat16 [4, 8, 8, 16, 1536], P('dp', 'expert'), may hold values from -6 to 6
- previous_right: bfloat16 [8, 1536, 128], P('expert', 'dp'), may hold values from -8 to 8
Outputs:
- left_factor: float32 [8, 5120, 128], P('expert', 'dp')
- right_factor: float32 [8, 1536, 128], P('expert', 'dp')
The draws below stay inside these ranges and needn't reach their ends.
Inputs may be any that keep to these rules, and one draw needn't show every extreme that they name: `token_experts`: each token names 6 different experts. On one device at most 16 tokens name any one of the experts 0 to 7, and in every draw one of these experts is named by exactly 16 tokens on every device.
All inputs are finite; a program needn't handle non-finite values.
Results may differ from the reference program's by a relative error of at most 0.0049.
Values may be sent and summed in bfloat16 or wider, within the bound.
No kernel may reach another device: no remote copies, remote signals or barrier semaphores. Data moves between devices by JAX's collectives and lax.ppermute only.
A program may use at most 64 MiB of HBM per device.

```python
import math
import jax
import jax.numpy as jnp
from jax import lax

D = 5120
FF = 1536
EXPERTS = 160
TOP = 6
RANK = 128
MOST = 16
TOK_DEV = 128
EXPERT_SPAN = 8
TOKENS = 4096
N_DP = 4
N_EXPERT = 8


def draw_token_experts(key, part):
    key = jax.random.fold_in(key, 11)
    random_subkeys = jax.random.split(key, 4)
    blocks = TOKENS // TOK_DEV
    favoured = jax.random.randint(random_subkeys[0], (), 0, EXPERT_SPAN)
    extra_boost = jax.random.randint(random_subkeys[1], (EXPERT_SPAN,), 400, 1400)
    opening = jax.random.randint(random_subkeys[2], (blocks, 1, EXPERT_SPAN), 0, TOK_DEV)
    router_scores = jax.random.randint(random_subkeys[3], (blocks, TOK_DEV, EXPERTS), 0, 1000)
    position = jnp.arange(TOK_DEV, dtype=jnp.int32)[None, :, None]
    allowed = (position - opening) % TOK_DEV < MOST
    within_range = router_scores[:, :, :EXPERT_SPAN] + extra_boost[None, None, :]
    within_range = jnp.where(jnp.arange(EXPERT_SPAN, dtype=jnp.int32)[None, None, :] == favoured, 1000000, within_range)
    within_range = jnp.where(allowed, within_range, -1000000)
    router_scores = jnp.concatenate([within_range, router_scores[:, :, EXPERT_SPAN:]], axis=2)
    router_scores = router_scores * 256 + jnp.arange(EXPERTS, dtype=jnp.int32)[None, None, :]
    ranked, chosen = lax.top_k(router_scores, TOP)
    return chosen.reshape(TOKENS, TOP).astype(jnp.int32)


def draw_previous_right(key, part):
    key = jax.random.fold_in(key, 23)
    random_subkeys = jax.random.split(key, 3)
    shared = jax.random.normal(random_subkeys[1], (EXPERT_SPAN, FF, 1), jnp.float32)
    mixing = jax.random.uniform(random_subkeys[2], (EXPERT_SPAN, 1, RANK), jnp.float32, 0.3, 0.8)
    noise = jax.random.normal(random_subkeys[0], (EXPERT_SPAN, FF, RANK), jnp.float32)
    return jnp.clip(noise + shared * mixing, -8.0, 8.0).astype(jnp.bfloat16)


def levels(own_key, shape, shards, low, top_value):
    def one(dim, blocks):
        draws = jax.random.uniform(jax.random.fold_in(jax.random.fold_in(own_key, 6), dim), (blocks,), jnp.float32, low / len(shards), top_value / len(shards))
        return jnp.repeat(jnp.exp(draws), shape[dim] // blocks).reshape((-1,) + (1,) * (len(shape) - dim - 1))

    gain = one(*shards[0])
    for cut in shards[1:]:
        gain = gain * one(*cut)
    return gain


def normal_values(rng, extent, width, bound, cuts=(), kind=jnp.bfloat16):
    drawn = jax.random.normal(rng, extent, jnp.float32) * width
    if len(cuts) > 0:
        drawn = levels(rng, extent, cuts, -0.22, 0.18) * drawn
    return jnp.clip(drawn, min=-bound, max=bound).astype(kind)


def setup_inputs(seed: int = 0) -> dict:
    key_of = jax.random.split(jax.random.key(seed), 6)
    cotangent = normal_values(key_of[0], (TOKENS, D), 1.0, 6.0, ((0, 32),))
    route_weights = jnp.clip(jnp.exp(math.log(1.0) - 2.9957323 * jax.random.uniform(key_of[1], (TOKENS, TOP), jnp.float32) ** levels(key_of[1], (TOKENS, TOP), ((0, 32),), -0.2, 0.2)), 0.05, 1.0)
    token_experts = draw_token_experts(jax.random.fold_in(key_of[5], 71), 0)
    saved_hidden = normal_values(key_of[3], (N_DP, EXPERT_SPAN, EXPERT_SPAN, MOST, FF), 1.0, 6.0, ((0, 4), (1, 8)))
    previous_right = draw_previous_right(jax.random.fold_in(key_of[5], 71), 0)
    return {"cotangent": cotangent, "route_weights": route_weights, "token_experts": token_experts, "saved_hidden": saved_hidden, "previous_right": previous_right}


EPSILON = 1e-06

def reference(cotangent, route_weights, token_experts, saved_hidden, previous_right):
    devices = N_DP * N_EXPERT
    cotangent_blocks = cotangent.reshape(devices, TOK_DEV, D)
    expert_blocks = token_experts.reshape(devices, TOK_DEV, TOP)
    weight_blocks = route_weights.reshape(devices, TOK_DEV, TOP)
    slot_range = jnp.arange(MOST, dtype=jnp.int32)
    token_range = jnp.arange(TOK_DEV, dtype=jnp.int32)

    def one_expert(expert):
        matches = expert_blocks == expert
        routed = jnp.any(matches, axis=2).astype(jnp.int32)
        weight_sum = lax.optimization_barrier(jnp.sum(jnp.where(matches, weight_blocks, 0.0), axis=2))
        slots = jnp.cumsum(routed, axis=1) - routed
        chosen = (routed[:, :, None] == 1) & (slots[:, :, None] == slot_range[None, None, :])
        source_row = lax.optimization_barrier(jnp.sum(jnp.where(chosen, token_range[None, :, None], 0), axis=1)).astype(jnp.int32)
        slot_weight = lax.optimization_barrier(jnp.sum(jnp.where(chosen, weight_sum[:, :, None], 0.0), axis=1))
        picked = jnp.take_along_axis(cotangent_blocks, source_row[:, :, None], axis=1)
        scaled_rows = (picked * slot_weight[:, :, None]).astype(jnp.bfloat16).reshape(devices * MOST, D)
        hidden_rows = lax.dynamic_index_in_dim(saved_hidden, expert, 1, keepdims=False).reshape(devices * MOST, FF)
        right_prev = lax.dynamic_index_in_dim(previous_right, expert, 0, keepdims=False)
        projected = jnp.dot(hidden_rows.astype(jnp.float32), right_prev.astype(jnp.float32), preferred_element_type=jnp.float32).astype(jnp.bfloat16)
        left_sum = jnp.dot(scaled_rows.T.astype(jnp.float32), projected.astype(jnp.float32), preferred_element_type=jnp.float32)
        basis, triangle = jnp.linalg.qr(left_sum)
        signs = jnp.where(jnp.diagonal(triangle) < 0, -1.0, 1.0)
        basis = basis * signs[None, :]
        rotated_factor = jnp.dot(scaled_rows.astype(jnp.float32), basis.astype(jnp.bfloat16).astype(jnp.float32), preferred_element_type=jnp.float32).astype(jnp.bfloat16)
        right_sum = jnp.dot(hidden_rows.T.astype(jnp.float32), rotated_factor.astype(jnp.float32), preferred_element_type=jnp.float32)
        column_sums = lax.optimization_barrier(jnp.sum(right_sum * right_sum, axis=0))
        left_out = basis * math.sqrt(D)
        right_out = right_sum * (math.sqrt(FF) / jnp.sqrt(column_sums + EPSILON))
        return (left_out, right_out)
    left_factor, right_factor = lax.map(one_expert, jnp.arange(N_EXPERT, dtype=jnp.int32))
    return (left_factor, right_factor)
```

```python
import math

import jax
import jax.numpy as jnp
from jax import lax
from jax.sharding import PartitionSpec as P

EPSILON = 1e-06
HIGHEST = lax.Precision.HIGHEST
CONTRACT_ROWS = (((0,), (0,)), ((), ()))


def inverse_upper(gram):
    lower = jnp.linalg.cholesky(gram)
    identity = jnp.eye(gram.shape[0], dtype=jnp.float32)
    return lax.linalg.triangular_solve(
        lower, identity, left_side=False, lower=True, transpose_a=True
    )


def sum_over_dp(value, shards):
    step = 1
    while step < shards:
        other = lax.ppermute(value, "dp", [(i, i ^ step) for i in range(shards)])
        value = value + other
        step *= 2
    return value


def local(cotangent, route_weights, token_experts, saved_hidden, previous_right):
    window = lax.axis_size("expert")
    shards = lax.axis_size("dp")
    position = lax.axis_index("dp")
    token_count, model_width = cotangent.shape
    capacity = saved_hidden.shape[3]
    hidden_width = saved_hidden.shape[4]
    own_columns = model_width // shards
    own_hidden = hidden_width // shards

    hidden_rows = lax.all_gather(
        saved_hidden.reshape(window * capacity, hidden_width), "dp", axis=0, tiled=True
    )
    right_whole = lax.all_gather(previous_right[0], "dp", axis=0, tiled=True)

    expert_range = jnp.arange(window, dtype=jnp.int32)
    matches = token_experts[:, :, None] == expert_range[None, None, :]
    routed = jnp.any(matches, axis=1).astype(jnp.int32)
    weight_sum = jnp.sum(jnp.where(matches, route_weights[:, :, None], 0.0), axis=1)
    slots = jnp.cumsum(routed, axis=0) - routed
    chosen = (routed[:, :, None] == 1) & (
        slots[:, :, None] == jnp.arange(capacity, dtype=jnp.int32)[None, None, :]
    )
    token_range = jnp.arange(token_count, dtype=jnp.int32)
    source_row = jnp.sum(jnp.where(chosen, token_range[:, None, None], 0), axis=0)
    slot_weight = jnp.sum(jnp.where(chosen, weight_sum[:, :, None], 0.0), axis=0)
    picked = jnp.take(cotangent, source_row.reshape(-1), axis=0).reshape(
        window * capacity, shards, own_columns
    )
    outgoing = (picked * slot_weight.reshape(-1)[:, None, None]).astype(jnp.bfloat16)
    outgoing = outgoing.transpose(1, 0, 2).reshape(shards * window, capacity, own_columns)
    arrived = lax.all_to_all(
        outgoing, ("dp", "expert"), split_axis=0, concat_axis=0, tiled=True
    ).reshape(shards * window * capacity, own_columns)

    projected = (
        jnp.dot(hidden_rows, right_whole, preferred_element_type=jnp.float32)
        .astype(jnp.bfloat16)
        .astype(jnp.float32)
    )
    inner = inverse_upper(
        lax.dot_general(
            projected, projected, CONTRACT_ROWS, precision=HIGHEST,
            preferred_element_type=jnp.float32,
        )
    )
    prepared = jnp.dot(projected, inner, precision=HIGHEST, preferred_element_type=jnp.float32)

    rows = arrived.astype(jnp.float32)
    left_part = lax.dot_general(
        rows, prepared, CONTRACT_ROWS, precision=HIGHEST, preferred_element_type=jnp.float32
    )
    gram = lax.dot_general(
        left_part, left_part, CONTRACT_ROWS, precision=HIGHEST,
        preferred_element_type=jnp.float32,
    )
    turned = jnp.dot(rows, left_part, precision=HIGHEST, preferred_element_type=jnp.float32)
    gram = sum_over_dp(gram, shards)
    turned = sum_over_dp(turned, shards)
    outer = inverse_upper(gram)
    left_out = jnp.dot(
        left_part, outer * math.sqrt(model_width), precision=HIGHEST,
        preferred_element_type=jnp.float32,
    )
    rotated = jnp.dot(turned, outer, precision=HIGHEST, preferred_element_type=jnp.float32)
    right_sum = lax.dot_general(
        hidden_rows.astype(jnp.float32), rotated, CONTRACT_ROWS, precision=HIGHEST,
        preferred_element_type=jnp.float32,
    )
    column_sums = jnp.sum(right_sum * right_sum, axis=0)
    right_own = lax.dynamic_slice_in_dim(right_sum, position * own_hidden, own_hidden, 0)
    right_out = right_own * (math.sqrt(hidden_width) / jnp.sqrt(column_sums + EPSILON))
    return (left_out[None], right_out[None])


def solution(mesh):
    in_specs = (
        P(("dp", "expert"), None),
        P(("dp", "expert"), None),
        P(("dp", "expert"), None),
        P("dp", "expert", None, None, None),
        P("expert", "dp", None),
    )
    out_specs = (P("expert", "dp", None), P("expert", "dp", None))
    return jax.shard_map(local, mesh=mesh, in_specs=in_specs, out_specs=out_specs, check_vma=False)
```
